512 devices in a mesh: space: 64 (over z_lo, y, core), filt: 8 (over x, z_hi).
Axes of the slice: x: 4, y: 8, z: 8 (z_hi: 2, z_lo: 4; z = z_hi * 4 + z_lo), core: 2. Of those that a mesh axis runs over, the one named last changes fastest.
Arguments:
- activations: bfloat16 [256, 131072], P(None, 'space'), may hold values from -6 to 6
- out_grad: bfloat16 [256, 131072], P('filt', 'space'), may hold values from -6 to 6
- kernel: bfloat16 [256, 3, 3, 256], P('filt'), may hold values from -0.125 to 0.125
Outputs:
- input_grad: bfloat16 [256, 131072], P('filt', 'space')
- weight_grad: float32 [256, 3, 3, 256], P('filt')
The draws below stay inside these ranges and needn't reach their ends.
All inputs are finite; a program needn't handle non-finite values.
Results may differ from the reference program's by a relative error of at most 0.015.
Values may be sent and summed in bfloat16 or wider, within the bound.
No kernel may reach another device: no remote copies, remote signals or barrier semaphores. Data moves between devices by JAX's collectives and lax.ppermute only.
A program may use at most 64 MiB of HBM per device.

```python
import math
import jax
import jax.numpy as jnp
from jax import lax

C = 256
F = 256
COLS = 1024
HEIGHT = 128
NPIX = 131072
N_FILT = 8


def block_scale(rng, dims, split, smallest, high):
    def one(axis_at, parts):
        heights = jax.random.uniform(jax.random.fold_in(jax.random.fold_in(rng, 6), axis_at), (parts,), jnp.float32, smallest / len(split), high / len(split))
        return jnp.repeat(jnp.exp(heights), dims[axis_at] // parts).reshape((-1,) + (1,) * (len(dims) - axis_at - 1))

    factor_of = one(*split[0])
    for cut in split[1:]:
        factor_of = factor_of * one(*cut)
    return factor_of


def gaussian(stream_key, dims, scale, most, split=(), held_as=jnp.bfloat16):
    values = jax.random.normal(stream_key, dims, jnp.float32) * scale
    if len(split) > 0:
        values = block_scale(stream_key, dims, split, -0.22, 0.18) * values
    return jnp.clip(values, min=-most, max=most).astype(held_as)


def setup_inputs(seed: int = 0) -> dict:
    key_of = jax.random.split(jax.random.key(seed), 4)
    activations = gaussian(key_of[0], (C, NPIX), 1.0, 6.0, ((1, 64),))
    out_grad = gaussian(key_of[1], (F, NPIX), 1.0, 6.0, ((0, 8), (1, 64)))
    kernel = gaussian(key_of[2], (F, 3, 3, C), (9 * C) ** -0.5, 0.125, ((0, 8),))
    return {"activations": activations, "out_grad": out_grad, "kernel": kernel}


def shift_map(field, row_step, col_step):
    padded = jnp.pad(field, ((0, 0), (1, 1), (1, 1)))
    return padded[:, 1 + row_step:1 + row_step + HEIGHT, 1 + col_step:1 + col_step + COLS]

def reference(activations, out_grad, kernel):
    inputs = activations.reshape(C, HEIGHT, COLS)
    grads = out_grad.reshape(F, HEIGHT, COLS)
    blocks = []
    for tap_row in range(3):
        for tap_col in range(3):
            moved = shift_map(inputs, tap_row - 1, tap_col - 1).reshape(C, NPIX)
            blocks.append(lax.dot_general(out_grad, moved, (((1,), (1,)), ((), ())), preferred_element_type=jnp.float32))
    weight_grad = jnp.stack(blocks, 1).reshape(F, 3, 3, C) * (1.0 / math.sqrt(NPIX))
    group = F // N_FILT
    total = jnp.zeros((C, NPIX), jnp.float32)
    for shard in range(N_FILT):
        partial_value = jnp.zeros((C, NPIX), jnp.float32)
        for tap_row in range(3):
            for tap_col in range(3):
                back = shift_map(grads[shard * group:(shard + 1) * group], 1 - tap_row, 1 - tap_col).reshape(group, NPIX)
                taps = kernel[shard * group:(shard + 1) * group, tap_row, tap_col, :]
                partial_value = partial_value + lax.dot_general(taps, back, (((0,), (0,)), ((), ())), preferred_element_type=jnp.float32)
        total = total + lax.optimization_barrier(partial_value.astype(jnp.bfloat16)).astype(jnp.float32)
    return (total.astype(jnp.bfloat16), weight_grad)
```

```python
import math

import jax
import jax.numpy as jnp
from jax import lax
from jax.sharding import PartitionSpec as P

COLS = 1024


def halo_rows(array):
    size = lax.axis_size("space")
    up = [(i, i + 1) for i in range(size - 1)]
    down = [(j, i) for i, j in up]
    before = lax.ppermute(array[:, -COLS:], "space", up)
    after = lax.ppermute(array[:, :COLS], "space", down)
    return before, after


def shifted_stack(out_grad, before, after):
    filters, pixels = out_grad.shape
    rows = jnp.concatenate([before, out_grad, after], axis=1)
    column = lax.broadcasted_iota(jnp.int32, (1, rows.shape[1]), 1) % COLS
    zero = jnp.zeros((), rows.dtype)
    right = jnp.where(column == 0, zero, jnp.roll(rows, 1, axis=1))
    left = jnp.where(column == COLS - 1, zero, jnp.roll(rows, -1, axis=1))
    by_col = {-1: right, 0: rows, 1: left}
    stack = []
    for i in range(3):
        for j in range(3):
            start = COLS * (2 - i)
            stack.append(by_col[1 - j][:, start:start + pixels])
    return jnp.concatenate(stack, axis=0)


def body(activations, out_grad, kernel):
    channels, pixels = activations.shape
    filters = out_grad.shape[0]
    n_space = lax.axis_size("space")
    n_filt = lax.axis_size("filt")
    scale = 1.0 / math.sqrt(pixels * n_space)
    before, after = halo_rows(out_grad)
    stack = shifted_stack(out_grad, before, after)
    terms = lax.dot_general(stack, activations, (((1,), (1,)), ((), ())), preferred_element_type=jnp.float32)
    terms = (terms * scale).astype(jnp.bfloat16)
    tiles = terms.reshape(36, 8, 2, 128).transpose(0, 2, 1, 3).reshape(72, 8, 128)
    low = tiles[:64]
    high = jnp.pad(tiles[64:], ((0, 56), (0, 0), (0, 0)))
    chunks = jnp.concatenate([low, high], axis=1)
    got = lax.all_to_all(chunks, "space", 0, 0, tiled=True)
    total = jnp.sum(got.astype(jnp.float32), axis=0).astype(jnp.bfloat16)
    everyone = jnp.broadcast_to(total[None], (n_space,) + total.shape)
    full = lax.all_to_all(everyone, "space", 0, 0, tiled=True)
    full = jnp.concatenate([full[:, :8], full[:8, 8:]], axis=0).astype(jnp.float32)
    weight = full.reshape(36, 2, 8, 128).transpose(0, 2, 1, 3).reshape(3, 3, filters, channels)
    weight_grad = weight.transpose(2, 0, 1, 3)

    taps = kernel.transpose(1, 2, 0, 3).reshape(9 * filters, channels)
    partial = lax.dot_general(taps, stack, (((0,), (0,)), ((), ())), preferred_element_type=jnp.float32)
    partial = partial.astype(jnp.bfloat16)
    shares = lax.all_to_all(partial, "filt", 0, 0, tiled=True).reshape(n_filt, channels // n_filt, pixels)
    input_grad = jnp.sum(shares.astype(jnp.float32), axis=0).astype(jnp.bfloat16)
    return (input_grad, weight_grad)


def solution(mesh):
    in_specs = (P(None, "space"), P("filt", "space"), P("filt", None, None, None))
    out_specs = (P("filt", "space"), P("filt", None, None, None))
    return jax.shard_map(body, mesh=mesh, in_specs=in_specs, out_specs=out_specs, check_vma=False)
```

```python
import math

import jax
import jax.numpy as jnp
from jax import lax
from jax.sharding import PartitionSpec as P

COLS = 1024


def halo_rows(array):
    size = lax.axis_size("space")
    up = [(i, i + 1) for i in range(size - 1)]
    down = [(j, i) for i, j in up]
    before = lax.ppermute(array[:, -COLS:], "space", up)
    after = lax.ppermute(array[:, :COLS], "space", down)
    return before, after


def shifted_stack(out_grad, before, after):
    filters, pixels = out_grad.shape
    rows = jnp.concatenate([before, out_grad, after], axis=1)
    column = lax.broadcasted_iota(jnp.int32, (1, rows.shape[1]), 1) % COLS
    zero = jnp.zeros((), rows.dtype)
    right = jnp.where(column == 0, zero, jnp.roll(rows, 1, axis=1))
    left = jnp.where(column == COLS - 1, zero, jnp.roll(rows, -1, axis=1))
    by_col = {-1: right, 0: rows, 1: left}
    stack = []
    for i in range(3):
        for j in range(3):
            start = COLS * (2 - i)
            stack.append(by_col[1 - j][:, start:start + pixels])
    return jnp.concatenate(stack, axis=0)


def body(activations, out_grad, kernel):
    channels, pixels = activations.shape
    filters = out_grad.shape[0]
    n_space = lax.axis_size("space")
    n_filt = lax.axis_size("filt")
    n_x = n_filt // 2
    scale = 1.0 / math.sqrt(pixels * n_space)
    before, after = halo_rows(out_grad)

    me = lax.axis_index("filt")
    here, half = me // 2, me % 2
    taps = kernel.transpose(3, 1, 2, 0).reshape(n_x, 2, channels // n_filt, 9 * filters)
    taps = lax.dynamic_slice_in_dim(jnp.concatenate([taps, taps], axis=0), here, n_x, axis=0)
    taps = jnp.where(half == 1, taps[:, ::-1], taps).reshape(n_x, 2 * (channels // n_filt), 9 * filters)

    stack = shifted_stack(out_grad, before, after)
    terms = lax.dot_general(stack, activations, (((1,), (1,)), ((), ())), preferred_element_type=jnp.float32)
    terms = (terms * scale).astype(jnp.bfloat16)
    tiles = terms.reshape(36, 8, 2, 128).transpose(0, 2, 1, 3).reshape(72, 8, 128)
    low = tiles[:64]
    high = jnp.pad(tiles[64:], ((0, 56), (0, 0), (0, 0)))
    chunks = jnp.concatenate([low, high], axis=1)
    got = lax.all_to_all(chunks, "space", 0, 0, tiled=True)

    own = None
    arrived = []
    for k in range(n_x):
        part = lax.dot_general(taps[k], stack, (((1,), (0,)), ((), ())), preferred_element_type=jnp.float32)
        part = part.astype(jnp.bfloat16)
        if k == 0:
            own = part
        else:
            pairs = [(i, (i + 2 * k) % n_filt) for i in range(n_filt)]
            arrived.append(lax.ppermute(part, "filt", pairs))

    total = jnp.sum(got.astype(jnp.float32), axis=0).astype(jnp.bfloat16)
    everyone = jnp.broadcast_to(total[None], (n_space,) + total.shape)
    full = lax.all_to_all(everyone, "space", 0, 0, tiled=True)

    summed = own.astype(jnp.float32)
    for other in arrived:
        summed = summed + other.astype(jnp.float32)
    keep, give = jnp.split(summed, 2, axis=0)
    swapped = lax.ppermute(give.astype(jnp.bfloat16), "filt", [(i, i ^ 1) for i in range(n_filt)])
    input_grad = (keep + swapped.astype(jnp.float32)).astype(jnp.bfloat16)

    full = jnp.concatenate([full[:, :8], full[:8, 8:]], axis=0).astype(jnp.float32)
    weight = full.reshape(36, 2, 8, 128).transpose(0, 2, 1, 3).reshape(3, 3, filters, channels)
    weight_grad = weight.transpose(2, 0, 1, 3)
    return (input_grad, weight_grad)


def solution(mesh):
    in_specs = (P(None, "space"), P("filt", "space"), P("filt", None, None, None))
    out_specs = (P("filt", "space"), P("filt", None, None, None))
    return jax.shard_map(body, mesh=mesh, in_specs=in_specs, out_specs=out_specs, check_vma=False)
```

```python
import functools
import math

import jax
import jax.numpy as jnp
from jax import lax
from jax.experimental import pallas as pl
from jax.experimental.pallas import tpu as pltpu
from jax.sharding import PartitionSpec as P

COLS = 1024
VMEM = pl.BlockSpec(memory_space=pltpu.VMEM)
SMEM = pl.BlockSpec(memory_space=pltpu.SMEM)


def cost(flops):
    return pl.CostEstimate(flops=flops, bytes_accessed=1 << 20, transcendentals=0)


def halo_rows(array):
    size = lax.axis_size("space")
    up = [(i, i + 1) for i in range(size - 1)]
    down = [(j, i) for i, j in up]
    before = lax.ppermute(array[:, -COLS:], "space", up)
    after = lax.ppermute(array[:, :COLS], "space", down)
    return before, after


def shifted_stack(out_grad, before, after):
    filters, pixels = out_grad.shape
    rows = jnp.concatenate([before, out_grad, after], axis=1)
    column = lax.broadcasted_iota(jnp.int32, (1, rows.shape[1]), 1) % COLS
    zero = jnp.zeros((), rows.dtype)
    right = jnp.where(column == 0, zero, jnp.roll(rows, 1, axis=1))
    left = jnp.where(column == COLS - 1, zero, jnp.roll(rows, -1, axis=1))
    by_col = {-1: right, 0: rows, 1: left}
    stack = []
    for i in range(3):
        for j in range(3):
            start = COLS * (2 - i)
            stack.append(by_col[1 - j][:, start:start + pixels])
    return jnp.concatenate(stack, axis=0)


def parts_kernel(n_x, share, where_ref, taps_ref, stack_ref, *rest):
    outs, turned, order = rest[:n_x], rest[n_x], rest[n_x + 1]
    turned[...] = taps_ref[...].astype(jnp.float32).T.astype(jnp.bfloat16)
    here, half = where_ref[0], where_ref[1]
    for k in range(n_x):
        block = lax.rem(here + k, n_x) * 2
        for h in range(2):
            start = pl.multiple_of((block + lax.rem(half + h, 2)) * share, share)
            order[(2 * k + h) * share:(2 * k + h + 1) * share, :] = turned[pl.ds(start, share), :]
    wide = 512
    for c in range(stack_ref.shape[1] // wide):
        cols = slice(c * wide, c * wide + wide)
        got = jnp.dot(order[...], stack_ref[:, cols], preferred_element_type=jnp.float32).astype(jnp.bfloat16)
        for k in range(n_x):
            outs[k][:, cols] = got[2 * k * share:2 * (k + 1) * share, :]


def sum_kernel(got_ref, out_ref):
    total = jnp.sum(got_ref[...].astype(jnp.float32), axis=0).astype(jnp.bfloat16)
    out_ref[...] = jnp.broadcast_to(total[None], out_ref.shape)


def weight_kernel(full_ref, out_ref):
    for d in range(72):
        row, col = d // 2, d % 2
        for g in range(4):
            pair = full_ref[d, g] if d < 64 else full_ref[(d - 64) * 4 + g, 4]
            top = row * 8 + 2 * g
            out_ref[top:top + 2, col * 128:col * 128 + 128] = pair.astype(jnp.float32)


def body(activations, out_grad, kernel):
    channels, pixels = activations.shape
    filters = out_grad.shape[0]
    n_space = lax.axis_size("space")
    n_filt = lax.axis_size("filt")
    n_x = n_filt // 2
    share = channels // n_filt
    scale = 1.0 / math.sqrt(pixels * n_space)
    before, after = halo_rows(out_grad)
    me = lax.axis_index("filt")
    where = jnp.stack([me // 2, me % 2])

    stack = shifted_stack(out_grad, before, after)
    terms = lax.dot_general(stack, activations, (((1,), (1,)), ((), ())), preferred_element_type=jnp.float32)
    terms = (terms * scale).astype(jnp.bfloat16)
    tiles = terms.reshape(36, 8, 2, 128).transpose(0, 2, 1, 3).reshape(72, 8, 128)
    low = tiles[:64].reshape(64, 4, 2, 128)
    high = jnp.pad(tiles[64:].reshape(32, 1, 2, 128), ((0, 32), (0, 0), (0, 0), (0, 0)))
    chunks = jnp.concatenate([low, high], axis=1)
    got = lax.all_to_all(chunks, "space", 0, 0, tiled=True)

    taps = kernel.transpose(1, 2, 0, 3).reshape(9 * filters, channels)
    part = jax.ShapeDtypeStruct((2 * share, pixels), jnp.bfloat16)
    own, *parts = pl.pallas_call(
        functools.partial(parts_kernel, n_x, share),
        out_shape=[part] * n_x,
        in_specs=[SMEM, VMEM, VMEM],
        out_specs=[VMEM] * n_x,
        scratch_shapes=[pltpu.VMEM((channels, 9 * filters), jnp.bfloat16)] * 2,
        cost_estimate=cost(P_COST),
        compiler_params=pltpu.CompilerParams(vmem_limit_bytes=32 << 20),
        name="parts",
    )(where, taps, stack)
    arrived = []
    for k in range(1, n_x):
        pairs = [(i, (i + 2 * k) % n_filt) for i in range(n_filt)]
        arrived.append(lax.ppermute(parts[k - 1], "filt", pairs))

    everyone = pl.pallas_call(
        sum_kernel,
        out_shape=jax.ShapeDtypeStruct(got.shape, jnp.bfloat16),
        in_specs=[VMEM], out_specs=VMEM, cost_estimate=cost(S_COST), name="chunk_sum",
    )(got)
    own, everyone = lax.optimization_barrier((own, everyone))
    full = lax.all_to_all(everyone, "space", 0, 0, tiled=True)

    summed = own.astype(jnp.float32)
    for other in arrived:
        summed = summed + other.astype(jnp.float32)
    keep, give = jnp.split(summed, 2, axis=0)
    swapped = lax.ppermute(give.astype(jnp.bfloat16), "filt", [(i, i ^ 1) for i in range(n_filt)])
    weight = pl.pallas_call(
        weight_kernel,
        out_shape=jax.ShapeDtypeStruct((9 * filters, channels), jnp.float32),
        in_specs=[VMEM], out_specs=VMEM, cost_estimate=cost(W_COST), name="weight_out",
    )(full)
    swapped, weight = lax.optimization_barrier((swapped, weight))
    input_grad = (keep + swapped.astype(jnp.float32)).astype(jnp.bfloat16)

    weight_grad = weight.reshape(3, 3, filters, channels).transpose(2, 0, 1, 3)
    return (input_grad, weight_grad)


P_COST = 115_000_000_000
S_COST = 115_000_000_000
W_COST = 115_000_000_000


def solution(mesh):
    in_specs = (P(None, "space"), P("filt", "space"), P("filt", None, None, None))
    out_specs = (P("filt", "space"), P("filt", None, None, None))
    return jax.shard_map(body, mesh=mesh, in_specs=in_specs, out_specs=out_specs, check_vma=False)
```

```python
import functools
import math

import jax
import jax.numpy as jnp
from jax import lax
from jax.experimental import pallas as pl
from jax.experimental.pallas import tpu as pltpu
from jax.sharding import PartitionSpec as P

COLS = 1024
VMEM = pl.BlockSpec(memory_space=pltpu.VMEM)
SMEM = pl.BlockSpec(memory_space=pltpu.SMEM)


def cost(flops):
    return pl.CostEstimate(flops=flops, bytes_accessed=1 << 20, transcendentals=0)


def halo_rows(array):
    size = lax.axis_size("space")
    up = [(i, i + 1) for i in range(size - 1)]
    down = [(j, i) for i, j in up]
    before = lax.ppermute(array[:, -COLS:], "space", up)
    after = lax.ppermute(array[:, :COLS], "space", down)
    return before, after


def put_line(stack_ref, line, at):
    filters, cols = line.shape
    column = lax.broadcasted_iota(jnp.int32, (filters, cols), 1)
    wide = line.astype(jnp.float32)
    left = jnp.where(column == cols - 1, 0.0, pltpu.roll(wide, cols - 1, 1)).astype(line.dtype)
    right = jnp.where(column == 0, 0.0, pltpu.roll(wide, 1, 1)).astype(line.dtype)
    for i in range(3):
        pixel_row = at - (2 - i)
        if 0 <= pixel_row < 2:
            for j, moved in enumerate((left, line, right)):
                top = (3 * i + j) * filters
                stack_ref[top:top + filters, pixel_row * cols:(pixel_row + 1) * cols] = moved


def inner_kernel(grad_ref, acts_ref, stack_ref, held_ref, sem):
    copy = pltpu.make_async_copy(acts_ref, held_ref, sem)
    copy.start()
    put_line(stack_ref, grad_ref[:, :COLS], 1)
    put_line(stack_ref, grad_ref[:, COLS:], 2)
    edge = jnp.zeros((3 * grad_ref.shape[0], COLS), stack_ref.dtype)
    stack_ref[0:edge.shape[0], COLS:] = edge
    stack_ref[2 * edge.shape[0]:, :COLS] = edge
    copy.wait()


def outer_kernel(scale, before_ref, after_ref, acts_ref, inner_ref, stack_ref, chunk_ref):
    put_line(stack_ref, before_ref[...], 0)
    put_line(stack_ref, after_ref[...], 3)
    terms = lax.dot_general(stack_ref[...], acts_ref[...], (((1,), (1,)), ((), ())), preferred_element_type=jnp.float32)
    terms = (terms * scale).astype(chunk_ref.dtype)
    for t in range(72):
        row, col = t // 2 * 8, t % 2 * 128
        chunk_ref[t] = terms[row:row + 8, col:col + 128]
    chunk_ref[72:80] = jnp.zeros((8, 8, 128), chunk_ref.dtype)


def parts_kernel(n_x, share, where_ref, taps_ref, stack_ref, *rest):
    outs, turned, order = rest[:n_x], rest[n_x], rest[n_x + 1]
    turned[...] = taps_ref[...].astype(jnp.float32).T.astype(jnp.bfloat16)
    here, half = where_ref[0], where_ref[1]
    for k in range(n_x):
        block = lax.rem(here + k, n_x) * 2
        for h in range(2):
            start = pl.multiple_of((block + lax.rem(half + h, 2)) * share, share)
            order[(2 * k + h) * share:(2 * k + h + 1) * share, :] = turned[pl.ds(start, share), :]
    wide = 512
    for c in range(stack_ref.shape[1] // wide):
        cols = slice(c * wide, c * wide + wide)
        got = jnp.dot(order[...], stack_ref[:, cols], preferred_element_type=jnp.float32).astype(jnp.bfloat16)
        for k in range(n_x):
            outs[k][:, cols] = got[2 * k * share:2 * (k + 1) * share, :]


def body(activations, out_grad, kernel):
    channels, pixels = activations.shape
    filters = out_grad.shape[0]
    n_space = lax.axis_size("space")
    n_filt = lax.axis_size("filt")
    n_x = n_filt // 2
    share = channels // n_filt
    scale = 1.0 / math.sqrt(pixels * n_space)
    before, after = halo_rows(out_grad)
    me = lax.axis_index("filt")
    where = jnp.stack([me // 2, me % 2])

    stack_type = jax.ShapeDtypeStruct((9 * filters, pixels), jnp.bfloat16)
    inner, held = pl.pallas_call(
        inner_kernel,
        out_shape=[stack_type, jax.ShapeDtypeStruct(activations.shape, activations.dtype)],
        in_specs=[VMEM, pl.BlockSpec(memory_space=pl.ANY)], out_specs=[VMEM, VMEM],
        scratch_shapes=[pltpu.SemaphoreType.DMA],
        cost_estimate=cost(4_000_000_000),
        compiler_params=pltpu.CompilerParams(vmem_limit_bytes=32 << 20),
        name="inner",
    )(out_grad, activations)
    stack, chunks = pl.pallas_call(
        functools.partial(outer_kernel, scale),
        out_shape=[stack_type, jax.ShapeDtypeStruct((80, 8, 128), jnp.bfloat16)],
        in_specs=[VMEM] * 4, out_specs=[VMEM] * 2, cost_estimate=cost(1_000_000_000),
        input_output_aliases={3: 0},
        compiler_params=pltpu.CompilerParams(vmem_limit_bytes=32 << 20),
        name="outer",
    )(before, after, held, inner)
    got = lax.all_to_all(chunks.reshape(64, 5, 2, 128), "space", 0, 0, tiled=True).reshape(chunks.shape)

    taps = kernel.transpose(1, 2, 0, 3).reshape(9 * filters, channels)
    part = jax.ShapeDtypeStruct((2 * share, pixels), jnp.bfloat16)
    own, *parts = pl.pallas_call(
        functools.partial(parts_kernel, n_x, share),
        out_shape=[part] * n_x,
        in_specs=[SMEM, VMEM, VMEM],
        out_specs=[VMEM] * n_x,
        scratch_shapes=[pltpu.VMEM((channels, 9 * filters), jnp.bfloat16)] * 2,
        cost_estimate=cost(P_COST),
        compiler_params=pltpu.CompilerParams(vmem_limit_bytes=32 << 20),
        name="parts",
    )(where, taps, stack)
    arrived = []
    for k in range(1, n_x):
        pairs = [(i, (i + 2 * k) % n_filt) for i in range(n_filt)]
        arrived.append(lax.ppermute(parts[k - 1], "filt", pairs))

    four = jnp.sum(got.reshape(16, 40, 128).astype(jnp.float32), axis=0)
    total = ((four[0:10] + four[10:20]) + (four[20:30] + four[30:40])).astype(jnp.bfloat16)
    everyone = jnp.broadcast_to(jnp.concatenate([total] * 4, axis=0)[None], (16, 40, 128))
    own, everyone = lax.optimization_barrier((own, everyone))
    full = lax.all_to_all(everyone.reshape(64, 5, 2, 128), "space", 0, 0, tiled=True).reshape(chunks.shape)

    summed = own.astype(jnp.float32)
    for other in arrived:
        summed = summed + other.astype(jnp.float32)
    keep, give = jnp.split(summed, 2, axis=0)
    swapped = lax.ppermute(give.astype(jnp.bfloat16), "filt", [(i, i ^ 1) for i in range(n_filt)])
    weight = full[:72].reshape(36, 2, 8, 128).transpose(0, 2, 1, 3).reshape(9 * filters, channels).astype(jnp.float32)
    swapped, weight = lax.optimization_barrier((swapped, weight))
    input_grad = (keep + swapped.astype(jnp.float32)).astype(jnp.bfloat16)

    weight_grad = weight.reshape(3, 3, filters, channels).transpose(2, 0, 1, 3)
    return (input_grad, weight_grad)


P_COST = 115_000_000_000


def solution(mesh):
    in_specs = (P(None, "space"), P("filt", "space"), P("filt", None, None, None))
    out_specs = (P("filt", "space"), P("filt", None, None, None))
    return jax.shard_map(body, mesh=mesh, in_specs=in_specs, out_specs=out_specs, check_vma=False)
```

```python
import functools
import math

import jax
import jax.numpy as jnp
from jax import lax
from jax.experimental import pallas as pl
from jax.experimental.pallas import tpu as pltpu
from jax.sharding import PartitionSpec as P

COLS = 1024
VMEM = pl.BlockSpec(memory_space=pltpu.VMEM)
SMEM = pl.BlockSpec(memory_space=pltpu.SMEM)


def cost(flops):
    return pl.CostEstimate(flops=flops, bytes_accessed=1 << 20, transcendentals=0)


def halo_rows(far, near):
    size = lax.axis_size("space")
    across = [(i, i + 1) for i in range(1, size - 1, 2)] + [(i + 1, i) for i in range(1, size - 1, 2)]
    return lax.ppermute(far, "space", across), lax.ppermute(near, "space", [(i, i ^ 1) for i in range(size)])


def put_line(stack_ref, line, at):
    filters, cols = line.shape
    column = lax.broadcasted_iota(jnp.int32, (filters, cols), 1)
    wide = line.astype(jnp.float32)
    left = jnp.where(column == cols - 1, 0.0, pltpu.roll(wide, cols - 1, 1)).astype(line.dtype)
    right = jnp.where(column == 0, 0.0, pltpu.roll(wide, 1, 1)).astype(line.dtype)
    for i in range(3):
        pixel_row = at - (2 - i)
        if 0 <= pixel_row < 2:
            for j, moved in enumerate((left, line, right)):
                top = (3 * i + j) * filters
                stack_ref[top:top + filters, pixel_row * cols:(pixel_row + 1) * cols] = moved


def line_kernel(core_ref, grad_ref, far_ref):
    far_ref[...] = grad_ref[:, pl.ds(pl.multiple_of(core_ref[0] * COLS, COLS), COLS)]


def inner_kernel(core_ref, grad_ref, near_ref, stack_ref):
    near_ref[...] = grad_ref[:, pl.ds(pl.multiple_of((1 - core_ref[0]) * COLS, COLS), COLS)]
    put_line(stack_ref, grad_ref[:, :COLS], 1)
    put_line(stack_ref, grad_ref[:, COLS:], 2)
    edge = jnp.zeros((3 * grad_ref.shape[0], COLS), stack_ref.dtype)
    stack_ref[0:edge.shape[0], COLS:] = edge
    stack_ref[2 * edge.shape[0]:, :COLS] = edge


def outer_kernel(scale, core_ref, far_ref, near_ref, acts_ref, inner_ref, stack_ref, chunk_ref):
    far, near = far_ref[...].astype(jnp.float32), near_ref[...].astype(jnp.float32)
    first_core = core_ref[0] == 0
    put_line(stack_ref, jnp.where(first_core, far, near).astype(far_ref.dtype), 0)
    put_line(stack_ref, jnp.where(first_core, near, far).astype(far_ref.dtype), 3)
    terms = lax.dot_general(stack_ref[...], acts_ref[...], (((1,), (1,)), ((), ())), preferred_element_type=jnp.float32)
    terms = (terms * scale).astype(chunk_ref.dtype)
    for t in range(72):
        row, col = t // 2 * 8, t % 2 * 128
        chunk_ref[t] = terms[row:row + 8, col:col + 128]
    chunk_ref[72:80] = jnp.zeros((8, 8, 128), chunk_ref.dtype)


def parts_kernel(n_x, share, where_ref, taps_ref, stack_ref, *rest):
    outs, turned, order = rest[:n_x], rest[n_x], rest[n_x + 1]
    turned[...] = taps_ref[...].astype(jnp.float32).T.astype(jnp.bfloat16)
    here, half = where_ref[0], where_ref[1]
    for k in range(n_x):
        block = lax.rem(here + k, n_x) * 2
        for h in range(2):
            start = pl.multiple_of((block + lax.rem(half + h, 2)) * share, share)
            order[(2 * k + h) * share:(2 * k + h + 1) * share, :] = turned[pl.ds(start, share), :]
    wide = 512
    for c in range(stack_ref.shape[1] // wide):
        cols = slice(c * wide, c * wide + wide)
        got = jnp.dot(order[...], stack_ref[:, cols], preferred_element_type=jnp.float32).astype(jnp.bfloat16)
        for k in range(n_x):
            outs[k][:, cols] = got[2 * k * share:2 * (k + 1) * share, :]


def body(activations, out_grad, kernel):
    channels, pixels = activations.shape
    filters = out_grad.shape[0]
    n_space = lax.axis_size("space")
    n_filt = lax.axis_size("filt")
    n_x = n_filt // 2
    share = channels // n_filt
    scale = 1.0 / math.sqrt(pixels * n_space)
    line_type = jax.ShapeDtypeStruct((filters, COLS), out_grad.dtype)
    core = (lax.axis_index("space") % 2).reshape(1)
    far = pl.pallas_call(
        line_kernel, out_shape=line_type, in_specs=[SMEM, VMEM], out_specs=VMEM, cost_estimate=cost(L_COST),
        compiler_params=pltpu.CompilerParams(vmem_limit_bytes=32 << 20), name="line",
    )(core, out_grad)
    me = lax.axis_index("filt")
    where = jnp.stack([me // 2, me % 2])

    stack_type = jax.ShapeDtypeStruct((9 * filters, pixels), jnp.bfloat16)
    near, inner = pl.pallas_call(
        inner_kernel, out_shape=[line_type, stack_type], in_specs=[SMEM, VMEM], out_specs=[VMEM] * 2,
        cost_estimate=cost(1_000_000), name="inner",
        compiler_params=pltpu.CompilerParams(vmem_limit_bytes=32 << 20),
    )(core, out_grad)
    far, near = halo_rows(far, near)
    stack, chunks = pl.pallas_call(
        functools.partial(outer_kernel, scale),
        out_shape=[stack_type, jax.ShapeDtypeStruct((80, 8, 128), jnp.bfloat16)],
        in_specs=[SMEM] + [VMEM] * 4, out_specs=[VMEM] * 2, cost_estimate=cost(1_000_000_000),
        input_output_aliases={4: 0},
        compiler_params=pltpu.CompilerParams(vmem_limit_bytes=32 << 20),
        name="outer",
    )(core, far, near, activations, inner)
    got = lax.all_to_all(chunks.reshape(64, 5, 2, 128), "space", 0, 0, tiled=True).reshape(chunks.shape)

    taps = kernel.transpose(1, 2, 0, 3).reshape(9 * filters, channels)
    part = jax.ShapeDtypeStruct((2 * share, pixels), jnp.bfloat16)
    own, *parts = pl.pallas_call(
        functools.partial(parts_kernel, n_x, share),
        out_shape=[part] * n_x,
        in_specs=[SMEM, VMEM, VMEM],
        out_specs=[VMEM] * n_x,
        scratch_shapes=[pltpu.VMEM((channels, 9 * filters), jnp.bfloat16)] * 2,
        cost_estimate=cost(P_COST),
        compiler_params=pltpu.CompilerParams(vmem_limit_bytes=32 << 20),
        name="parts",
    )(where, taps, stack)
    arrived = []
    for k in range(1, n_x):
        pairs = [(i, (i + 2 * k) % n_filt) for i in range(n_filt)]
        arrived.append(lax.ppermute(parts[k - 1], "filt", pairs))

    four = jnp.sum(got.reshape(16, 40, 128).astype(jnp.float32), axis=0)
    total = ((four[0:10] + four[10:20]) + (four[20:30] + four[30:40])).astype(jnp.bfloat16)
    everyone = jnp.broadcast_to(jnp.concatenate([total] * 4, axis=0)[None], (16, 40, 128))
    own, everyone = lax.optimization_barrier((own, everyone))
    full = lax.all_to_all(everyone.reshape(64, 5, 2, 128), "space", 0, 0, tiled=True).reshape(chunks.shape)

    summed = own.astype(jnp.float32)
    for other in arrived:
        summed = summed + other.astype(jnp.float32)
    keep, give = jnp.split(summed, 2, axis=0)
    swapped = lax.ppermute(give.astype(jnp.bfloat16), "filt", [(i, i ^ 1) for i in range(n_filt)])
    weight = full[:72].reshape(36, 2, 8, 128).transpose(0, 2, 1, 3).reshape(9 * filters, channels).astype(jnp.float32)
    swapped, weight = lax.optimization_barrier((swapped, weight))
    input_grad = (keep + swapped.astype(jnp.float32)).astype(jnp.bfloat16)

    weight_grad = weight.reshape(3, 3, filters, channels).transpose(2, 0, 1, 3)
    return (input_grad, weight_grad)


P_COST = 115_000_000_000
L_COST = 115_000_000_000


def solution(mesh):
    in_specs = (P(None, "space"), P("filt", "space"), P("filt", None, None, None))
    out_specs = (P("filt", "space"), P("filt", None, None, None))
    return jax.shard_map(body, mesh=mesh, in_specs=in_specs, out_specs=out_specs, check_vma=False)
```

```python
import functools
import math

import jax
import jax.numpy as jnp
from jax import lax
from jax.experimental import pallas as pl
from jax.experimental.pallas import tpu as pltpu
from jax.sharding import PartitionSpec as P

COLS = 1024
VMEM = pl.BlockSpec(memory_space=pltpu.VMEM)
SMEM = pl.BlockSpec(memory_space=pltpu.SMEM)


def cost(flops):
    return pl.CostEstimate(flops=flops, bytes_accessed=1 << 20, transcendentals=0)


def halo_rows(far, near):
    size = lax.axis_size("space")
    across = [(i, i + 1) for i in range(1, size - 1, 2)] + [(i + 1, i) for i in range(1, size - 1, 2)]
    return lax.ppermute(far, "space", across), lax.ppermute(near, "space", [(i, i ^ 1) for i in range(size)])


def put_line(stack_ref, line, at):
    filters, cols = line.shape
    column = lax.broadcasted_iota(jnp.int32, (filters, cols), 1)
    wide = line.astype(jnp.float32)
    left = jnp.where(column == cols - 1, 0.0, pltpu.roll(wide, cols - 1, 1)).astype(line.dtype)
    right = jnp.where(column == 0, 0.0, pltpu.roll(wide, 1, 1)).astype(line.dtype)
    for i in range(3):
        pixel_row = at - (2 - i)
        if 0 <= pixel_row < 2:
            for j, moved in enumerate((left, line, right)):
                top = (3 * i + j) * filters
                stack_ref[top:top + filters, pixel_row * cols:(pixel_row + 1) * cols] = moved


def line_kernel(core_ref, grad_ref, far_ref):
    far_ref[...] = grad_ref[:, pl.ds(pl.multiple_of(core_ref[0] * COLS, COLS), COLS)]


def inner_kernel(core_ref, grad_ref, near_ref, stack_ref):
    near_ref[...] = grad_ref[:, pl.ds(pl.multiple_of((1 - core_ref[0]) * COLS, COLS), COLS)]
    put_line(stack_ref, grad_ref[:, :COLS], 1)
    put_line(stack_ref, grad_ref[:, COLS:], 2)
    edge = jnp.zeros((3 * grad_ref.shape[0], COLS), stack_ref.dtype)
    stack_ref[0:edge.shape[0], COLS:] = edge
    stack_ref[2 * edge.shape[0]:, :COLS] = edge


def outer_kernel(scale, core_ref, far_ref, near_ref, acts_ref, inner_ref, stack_ref, chunk_ref):
    far, near = far_ref[...].astype(jnp.float32), near_ref[...].astype(jnp.float32)
    first_core = core_ref[0] == 0
    put_line(stack_ref, jnp.where(first_core, far, near).astype(far_ref.dtype), 0)
    put_line(stack_ref, jnp.where(first_core, near, far).astype(far_ref.dtype), 3)
    terms = lax.dot_general(stack_ref[...], acts_ref[...], (((1,), (1,)), ((), ())), preferred_element_type=jnp.float32)
    terms = (terms * scale).astype(chunk_ref.dtype)
    for t in range(72):
        row, col = t // 2 * 8, t % 2 * 128
        chunk_ref[t] = terms[row:row + 8, col:col + 128]
    chunk_ref[72:80] = jnp.zeros((8, 8, 128), chunk_ref.dtype)


def parts_kernel(n_x, share, where_ref, taps_ref, stack_ref, *rest):
    outs, turned, order = rest[:n_x], rest[n_x], rest[n_x + 1]
    turned[...] = taps_ref[...].astype(jnp.float32).T.astype(jnp.bfloat16)
    here, half = where_ref[0], where_ref[1]
    for k in range(n_x):
        block = lax.rem(here + k, n_x) * 2
        for h in range(2):
            start = pl.multiple_of((block + lax.rem(half + h, 2)) * share, share)
            order[(2 * k + h) * share:(2 * k + h + 1) * share, :] = turned[pl.ds(start, share), :]
    wide = 512
    for c in range(stack_ref.shape[1] // wide):
        cols = slice(c * wide, c * wide + wide)
        got = jnp.dot(order[...], stack_ref[:, cols], preferred_element_type=jnp.float32).astype(jnp.bfloat16)
        for k in range(n_x):
            outs[k][:, cols] = got[2 * k * share:2 * (k + 1) * share, :]


def body(activations, out_grad, kernel):
    channels, pixels = activations.shape
    filters = out_grad.shape[0]
    n_space = lax.axis_size("space")
    n_filt = lax.axis_size("filt")
    n_x = n_filt // 2
    share = channels // n_filt
    scale = 1.0 / math.sqrt(pixels * n_space)
    line_type = jax.ShapeDtypeStruct((filters, COLS), out_grad.dtype)
    core = (lax.axis_index("space") % 2).reshape(1)
    far = pl.pallas_call(
        line_kernel, out_shape=line_type, in_specs=[SMEM, VMEM], out_specs=VMEM, cost_estimate=cost(L_COST),
        compiler_params=pltpu.CompilerParams(vmem_limit_bytes=32 << 20), name="line",
    )(core, out_grad)
    me = lax.axis_index("filt")
    where = jnp.stack([me // 2, me % 2])

    stack_type = jax.ShapeDtypeStruct((9 * filters, pixels), jnp.bfloat16)
    near, inner = pl.pallas_call(
        inner_kernel, out_shape=[line_type, stack_type], in_specs=[SMEM, VMEM], out_specs=[VMEM] * 2,
        cost_estimate=cost(1_000_000), name="inner",
        compiler_params=pltpu.CompilerParams(vmem_limit_bytes=32 << 20),
    )(core, out_grad)
    far, near = halo_rows(far, near)
    stack, chunks = pl.pallas_call(
        functools.partial(outer_kernel, scale),
        out_shape=[stack_type, jax.ShapeDtypeStruct((80, 8, 128), jnp.bfloat16)],
        in_specs=[SMEM] + [VMEM] * 4, out_specs=[VMEM] * 2, cost_estimate=cost(1_000_000_000),
        input_output_aliases={4: 0},
        compiler_params=pltpu.CompilerParams(vmem_limit_bytes=32 << 20),
        name="outer",
    )(core, far, near, activations, inner)
    ring = [list(range(n_space // 4, n_space // 2)) + list(range(n_space // 4)) + list(range(n_space // 2, n_space))]
    got = lax.all_to_all(
        chunks.reshape(64, 5, 2, 128), "space", 0, 0, tiled=True, axis_index_groups=ring
    ).reshape(chunks.shape)

    taps = kernel.transpose(1, 2, 0, 3).reshape(9 * filters, channels)
    part = jax.ShapeDtypeStruct((2 * share, pixels), jnp.bfloat16)
    own, *parts = pl.pallas_call(
        functools.partial(parts_kernel, n_x, share),
        out_shape=[part] * n_x,
        in_specs=[SMEM, VMEM, VMEM],
        out_specs=[VMEM] * n_x,
        scratch_shapes=[pltpu.VMEM((channels, 9 * filters), jnp.bfloat16)] * 2,
        cost_estimate=cost(P_COST),
        compiler_params=pltpu.CompilerParams(vmem_limit_bytes=32 << 20),
        name="parts",
    )(where, taps, stack)
    arrived = []
    for k in range(1, n_x):
        pairs = [(i, (i + 2 * k) % n_filt) for i in range(n_filt)]
        arrived.append(lax.ppermute(parts[k - 1], "filt", pairs))

    four = jnp.sum(got.reshape(16, 40, 128).astype(jnp.float32), axis=0)
    total = ((four[0:10] + four[10:20]) + (four[20:30] + four[30:40])).astype(jnp.bfloat16)
    everyone = jnp.broadcast_to(jnp.concatenate([total] * 4, axis=0)[None], (16, 40, 128))
    own, everyone = lax.optimization_barrier((own, everyone))
    full = lax.all_to_all(
        everyone.reshape(64, 5, 2, 128), "space", 0, 0, tiled=True, axis_index_groups=ring
    ).reshape(chunks.shape)

    summed = own.astype(jnp.float32)
    for other in arrived:
        summed = summed + other.astype(jnp.float32)
    keep, give = jnp.split(summed, 2, axis=0)
    swapped = lax.ppermute(give.astype(jnp.bfloat16), "filt", [(i, i ^ 1) for i in range(n_filt)])
    weight = full[:72].reshape(36, 2, 8, 128).transpose(0, 2, 1, 3).reshape(9 * filters, channels).astype(jnp.float32)
    swapped, weight = lax.optimization_barrier((swapped, weight))
    input_grad = (keep + swapped.astype(jnp.float32)).astype(jnp.bfloat16)

    weight_grad = weight.reshape(3, 3, filters, channels).transpose(2, 0, 1, 3)
    return (input_grad, weight_grad)


P_COST = 115_000_000_000
L_COST = 115_000_000_000


def solution(mesh):
    in_specs = (P(None, "space"), P("filt", "space"), P("filt", None, None, None))
    out_specs = (P("filt", "space"), P("filt", None, None, None))
    return jax.shard_map(body, mesh=mesh, in_specs=in_specs, out_specs=out_specs, check_vma=False)
```

```python
import functools
import math

import jax
import jax.numpy as jnp
from jax import lax
from jax.experimental import pallas as pl
from jax.experimental.pallas import tpu as pltpu
from jax.sharding import PartitionSpec as P

COLS = 1024
VMEM = pl.BlockSpec(memory_space=pltpu.VMEM)
SMEM = pl.BlockSpec(memory_space=pltpu.SMEM)


def cost(flops):
    return pl.CostEstimate(flops=flops, bytes_accessed=1 << 20, transcendentals=0)


def halo_rows(far, near):
    size = lax.axis_size("space")
    across = [(i, i + 1) for i in range(1, size - 1, 2)] + [(i + 1, i) for i in range(1, size - 1, 2)]
    return lax.ppermute(far, "space", across), lax.ppermute(near, "space", [(i, i ^ 1) for i in range(size)])


def put_line(stack_ref, line, at):
    filters, cols = line.shape
    column = lax.broadcasted_iota(jnp.int32, (filters, cols), 1)
    wide = line.astype(jnp.float32)
    left = jnp.where(column == cols - 1, 0.0, pltpu.roll(wide, cols - 1, 1)).astype(line.dtype)
    right = jnp.where(column == 0, 0.0, pltpu.roll(wide, 1, 1)).astype(line.dtype)
    for i in range(3):
        pixel_row = at - (2 - i)
        if 0 <= pixel_row < 2:
            for j, moved in enumerate((left, line, right)):
                top = (3 * i + j) * filters
                stack_ref[top:top + filters, pixel_row * cols:(pixel_row + 1) * cols] = moved


def line_kernel(core_ref, grad_ref, far_ref):
    far_ref[...] = grad_ref[:, pl.ds(pl.multiple_of(core_ref[0] * COLS, COLS), COLS)]


def inner_kernel(core_ref, grad_ref, near_ref, stack_ref):
    near_ref[...] = grad_ref[:, pl.ds(pl.multiple_of((1 - core_ref[0]) * COLS, COLS), COLS)]
    put_line(stack_ref, grad_ref[:, :COLS], 1)
    put_line(stack_ref, grad_ref[:, COLS:], 2)
    edge = jnp.zeros((3 * grad_ref.shape[0], COLS), stack_ref.dtype)
    stack_ref[0:edge.shape[0], COLS:] = edge
    stack_ref[2 * edge.shape[0]:, :COLS] = edge


def outer_kernel(scale, core_ref, far_ref, near_ref, acts_ref, inner_ref, stack_ref, chunk_ref):
    far, near = far_ref[...].astype(jnp.float32), near_ref[...].astype(jnp.float32)
    first_core = core_ref[0] == 0
    put_line(stack_ref, jnp.where(first_core, far, near).astype(far_ref.dtype), 0)
    put_line(stack_ref, jnp.where(first_core, near, far).astype(far_ref.dtype), 3)
    terms = lax.dot_general(stack_ref[...], acts_ref[...], (((1,), (1,)), ((), ())), preferred_element_type=jnp.float32)
    terms = (terms * scale).astype(chunk_ref.dtype)
    for t in range(72):
        row, col = t // 2 * 8, t % 2 * 128
        chunk_ref[t] = terms[row:row + 8, col:col + 128]
    chunk_ref[72:80] = jnp.zeros((8, 8, 128), chunk_ref.dtype)


def parts_kernel(n_x, share, where_ref, taps_ref, stack_ref, *rest):
    outs, turned, order = rest[:n_x], rest[n_x], rest[n_x + 1]
    turned[...] = taps_ref[...].astype(jnp.float32).T.astype(jnp.bfloat16)
    here, half = where_ref[0], where_ref[1]
    for k in range(n_x):
        block = lax.rem(here + k, n_x) * 2
        for h in range(2):
            start = pl.multiple_of((block + lax.rem(half + h, 2)) * share, share)
            order[(2 * k + h) * share:(2 * k + h + 1) * share, :] = turned[pl.ds(start, share), :]
    wide = 512
    for c in range(stack_ref.shape[1] // wide):
        cols = slice(c * wide, c * wide + wide)
        got = jnp.dot(order[...], stack_ref[:, cols], preferred_element_type=jnp.float32).astype(jnp.bfloat16)
        for k in range(n_x):
            outs[k][:, cols] = got[2 * k * share:2 * (k + 1) * share, :]


def body(activations, out_grad, kernel):
    channels, pixels = activations.shape
    filters = out_grad.shape[0]
    n_space = lax.axis_size("space")
    n_filt = lax.axis_size("filt")
    n_x = n_filt // 2
    share = channels // n_filt
    scale = 1.0 / math.sqrt(pixels * n_space)
    line_type = jax.ShapeDtypeStruct((filters, COLS), out_grad.dtype)
    core = (lax.axis_index("space") % 2).reshape(1)
    far = pl.pallas_call(
        line_kernel, out_shape=line_type, in_specs=[SMEM, VMEM], out_specs=VMEM, cost_estimate=cost(L_COST),
        compiler_params=pltpu.CompilerParams(vmem_limit_bytes=32 << 20), name="line",
    )(core, out_grad)
    me = lax.axis_index("filt")
    where = jnp.stack([me // 2, me % 2])

    stack_type = jax.ShapeDtypeStruct((9 * filters, pixels), jnp.bfloat16)
    near, inner = pl.pallas_call(
        inner_kernel, out_shape=[line_type, stack_type], in_specs=[SMEM, VMEM], out_specs=[VMEM] * 2,
        cost_estimate=cost(1_000_000), name="inner",
        compiler_params=pltpu.CompilerParams(vmem_limit_bytes=32 << 20),
    )(core, out_grad)
    far, near = halo_rows(far, near)
    stack, chunks = pl.pallas_call(
        functools.partial(outer_kernel, scale),
        out_shape=[stack_type, jax.ShapeDtypeStruct((80, 8, 128), jnp.bfloat16)],
        in_specs=[SMEM] + [VMEM] * 4, out_specs=[VMEM] * 2, cost_estimate=cost(1_000_000_000),
        input_output_aliases={4: 0},
        compiler_params=pltpu.CompilerParams(vmem_limit_bytes=32 << 20),
        name="outer",
    )(core, far, near, activations, inner)
    middle = n_space // 2
    ring = [list(range(middle, n_space)) + list(range(middle))]
    got = lax.all_to_all(
        chunks.reshape(64, 5, 2, 128), "space", 0, 0, tiled=True, axis_index_groups=ring
    ).reshape(chunks.shape)

    taps = kernel.transpose(1, 2, 0, 3).reshape(9 * filters, channels)
    part = jax.ShapeDtypeStruct((2 * share, pixels), jnp.bfloat16)
    own, *parts = pl.pallas_call(
        functools.partial(parts_kernel, n_x, share),
        out_shape=[part] * n_x,
        in_specs=[SMEM, VMEM, VMEM],
        out_specs=[VMEM] * n_x,
        scratch_shapes=[pltpu.VMEM((channels, 9 * filters), jnp.bfloat16)] * 2,
        cost_estimate=cost(P_COST),
        compiler_params=pltpu.CompilerParams(vmem_limit_bytes=32 << 20),
        name="parts",
    )(where, taps, stack)
    arrived = []
    for k in range(1, n_x):
        pairs = [(i, (i + 2 * k) % n_filt) for i in range(n_filt)]
        arrived.append(lax.ppermute(parts[k - 1], "filt", pairs))

    four = jnp.sum(got.reshape(16, 40, 128).astype(jnp.float32), axis=0)
    total = ((four[0:10] + four[10:20]) + (four[20:30] + four[30:40])).astype(jnp.bfloat16)
    everyone = jnp.broadcast_to(jnp.concatenate([total] * 4, axis=0)[None], (16, 40, 128))
    own, everyone = lax.optimization_barrier((own, everyone))
    full = lax.all_to_all(
        everyone.reshape(64, 5, 2, 128), "space", 0, 0, tiled=True, axis_index_groups=ring
    ).reshape(chunks.shape)

    summed = own.astype(jnp.float32)
    for other in arrived:
        summed = summed + other.astype(jnp.float32)
    keep, give = jnp.split(summed, 2, axis=0)
    swapped = lax.ppermute(give.astype(jnp.bfloat16), "filt", [(i, i ^ 1) for i in range(n_filt)])
    weight = full[:72].reshape(36, 2, 8, 128).transpose(0, 2, 1, 3).reshape(9 * filters, channels).astype(jnp.float32)
    swapped, weight = lax.optimization_barrier((swapped, weight))
    input_grad = (keep + swapped.astype(jnp.float32)).astype(jnp.bfloat16)

    weight_grad = weight.reshape(3, 3, filters, channels).transpose(2, 0, 1, 3)
    return (input_grad, weight_grad)


P_COST = 115_000_000_000
L_COST = 115_000_000_000


def solution(mesh):
    in_specs = (P(None, "space"), P("filt", "space"), P("filt", None, None, None))
    out_specs = (P("filt", "space"), P("filt", None, None, None))
    return jax.shard_map(body, mesh=mesh, in_specs=in_specs, out_specs=out_specs, check_vma=False)
```
